32 devices in a mesh: pop: 8 (over z, y), tp: 4 (over x, core).
Axes of the slice: x: 2, y: 2, z: 4, core: 2. Of those that a mesh axis runs over, the one named last changes fastest.
Arguments:
- tokens: int32 [6, 24], replicated, may hold values from 0 to 65535
- embedding: bfloat16 [65536, 8192], P(('pop', 'tp')), may hold values from -6 to 6
- norm_gain: float32 [8192], replicated, may hold values from 0.1 to 1.9
- query_weight: bfloat16 [8192, 8192], P('pop', 'tp'), may hold values from -1 to 1
- out_weight: bfloat16 [8192, 8192], P('tp', 'pop'), may hold values from -0.0625 to 0.0625
- center: float32 [2, 8192, 1024], P(None, 'pop', 'tp'), may hold values from -6 to 6
- variance: float32 [2, 8192, 1024], P(None, 'pop', 'tp'), may hold values from 0.25 to 4
- step_path: float32 [2, 8192, 1024], P(None, 'pop', 'tp'), may hold values from -8 to 8
- spread_path: float32 [2, 8192, 1024], P(None, 'pop', 'tp'), may hold values from -6 to 6
- step_size: float32 [1], replicated, may hold values from 0.3 to 0.9
- noise_seeds: int32 [8], replicated, may hold values from 0 to 1073741823
- counters: int32 [8], replicated, may hold values from 0 to 1073741823
- fitness_rank: int32 [8], replicated, may hold values from 0 to 7, each once
Outputs:
- candidate_out: bfloat16 [8, 144, 8192], P('pop', None, 'tp')
- center_next: float32 [2, 8192, 1024], P(None, 'pop', 'tp')
- variance_next: float32 [2, 8192, 1024], P(None, 'pop', 'tp')
- step_path_next: float32 [2, 8192, 1024], P(None, 'pop', 'tp')
- spread_path_next: float32 [2, 8192, 1024], P(None, 'pop', 'tp')
- step_next: float32 [1], replicated
The draws below stay inside these ranges and needn't reach their ends.
Inputs may be any that keep to these rules, and one draw needn't show every extreme that they name: `fitness_rank`: each of 0 to 7 once.
All inputs are finite; a program needn't handle non-finite values.
Results may differ from the reference program's by a relative error of at most 0.04.
Values may be sent and summed in bfloat16 or wider, within the bound.
A program may use at most 192 MiB of HBM per device.

```python
import math
import jax
import jax.numpy as jnp
import numpy as np
from jax import lax

D = 8192
KV = 8
HD = 128
HQ = 64
VOCAB = 65536
LEN = 24
SEQS = 6
POP = 8
QW = 8192
KVW = 1024
N_TP = 4


def draw_query_weight(key, part):
    base_key = jax.random.fold_in(jax.random.fold_in(key, 11), 0)
    values = jax.random.truncated_normal(base_key, -6.0, 6.0, (D, QW), jnp.float32) * D ** (-0.5)
    return jnp.clip(values, -1.0, 1.0).astype(jnp.bfloat16)


def draw_step_path(key, part):
    row_key, col_key, base_key, pick_key, level_key = jax.random.split(jax.random.fold_in(key, 23), 5)
    row_scale = jnp.exp(jax.random.uniform(row_key, (D,), jnp.float32, 0.0, math.log(10.0))) / 4.6
    col_scale = jnp.exp(jax.random.uniform(col_key, (KVW,), jnp.float32, 0.0, math.log(10.0))) / 4.6
    row_place = lax.iota(jnp.int32, D).astype(jnp.float32) / D
    col_place = lax.iota(jnp.int32, KVW).astype(jnp.float32) / (KVW * POP)
    ramp = 1.0 + 2.0 * (row_place[:, None] + col_place[None, :])
    dominant = jax.random.randint(pick_key, (), 0, N_TP)
    others = jax.random.uniform(level_key, (N_TP,), jnp.float32, 0.8, 1.2)
    group_levels = jnp.where(lax.iota(jnp.int32, N_TP) == dominant, jnp.float32(2.5), others)
    col_group = lax.iota(jnp.int32, KVW) * N_TP // KVW
    col_level = jnp.take(group_levels, col_group)
    base = jax.random.truncated_normal(base_key, -6.0, 6.0, (2, D, KVW), jnp.float32)
    values = 0.4 * base * row_scale[None, :, None] * (col_scale * col_level)[None, None, :] * ramp[None]
    return jnp.clip(values, -8.0, 8.0)


def touch_ends(array, own_key, low, largest):
    shape = array.shape
    place = [jax.random.randint(jax.random.fold_in(own_key, axis), (), 0, shape[axis]) for axis in range(len(shape))]
    array = array.at[tuple(place)].set(low)
    longest = shape.index(max(shape))
    place[longest] = (place[longest] + 1) % shape[longest]
    return array.at[tuple(place)].set(largest)


def block_scale(own_key, dims, cuts, low, top_value):
    factor_of = 1.0
    for position, parts in cuts:
        steps = jax.random.uniform(jax.random.fold_in(jax.random.fold_in(own_key, 6), position), (parts,), jnp.float32, low / len(cuts), top_value / len(cuts))
        factor_of = factor_of * jnp.repeat(jnp.exp(steps), dims[position] // parts).reshape((-1,) + (1,) * (len(dims) - 1 - position))
    return factor_of


def cumulative_ranks(count, slope):
    portions = [(1 << 20) // math.isqrt(rank ** slope) + 1 for rank in range(1, count + 1)]
    deviation = 1 + sum(portions) // (1 << 30)
    return np.cumsum(np.array([max(1, weight // deviation) for weight in portions]))


def ranked_ids(rng, dims, count, skew):
    listing = cumulative_ranks(count, skew)
    pick = jax.random.randint(jax.random.fold_in(rng, 1), dims, 0, int(listing[count - 1]))
    grade = jnp.searchsorted(jnp.asarray(listing, jnp.int32), pick, side="right")
    return jax.random.permutation(jax.random.fold_in(rng, 2), count)[grade].astype(jnp.int32)


def gaussian(rng, dims, scale, limit, pieces=(), held_as=jnp.bfloat16):
    drawn = jax.random.normal(rng, dims, jnp.float32) * scale
    if len(pieces) > 0:
        drawn = block_scale(rng, dims, pieces, -0.22, 0.18) * drawn
    return jnp.clip(drawn, min=-limit, max=limit).astype(held_as)


def setup_inputs(seed: int = 0) -> dict:
    seeds = jax.random.split(jax.random.key(seed), 14)
    return {
        "tokens": touch_ends(ranked_ids(seeds[0], (SEQS, LEN), VOCAB, 2), jax.random.fold_in(seeds[0], 3), 0, VOCAB - 1).astype(jnp.int32),
        "embedding": gaussian(seeds[1], (VOCAB, D), 1.0, 6.0, ((0, 32),)),
        "norm_gain": jnp.clip(1.0 + 0.18 * jax.random.normal(seeds[2], (D,), jnp.float32), 0.1, 1.9),
        "query_weight": draw_query_weight(jax.random.fold_in(seeds[13], 71), 0),
        "out_weight": gaussian(seeds[4], (QW, D), QW ** -0.5, 0.0625, ((0, 4), (1, 8))),
        "center": gaussian(seeds[5], (2, D, KVW), 1.0, 6.0, ((1, 8), (2, 4)), jnp.float32),
        "variance": jnp.clip(jnp.exp(math.log(4.0) - 2.7725887 * jax.random.uniform(seeds[6], (2, D, KVW), jnp.float32) ** block_scale(seeds[6], (2, D, KVW), ((1, 8), (2, 4)), -0.2, 0.2)), 0.25, 4.0),
        "step_path": draw_step_path(jax.random.fold_in(seeds[13], 71), 0),
        "spread_path": gaussian(seeds[8], (2, D, KVW), 1.0, 6.0, ((1, 8), (2, 4)), jnp.float32),
        "step_size": jnp.clip(jax.random.uniform(seeds[9], (1,), jnp.float32, 0.3, 0.9), 0.3, 0.9),
        "noise_seeds": touch_ends(jax.random.randint(seeds[10], (POP,), 0, 1073741824), jax.random.fold_in(seeds[10], 1), 0, 1073741823).astype(jnp.int32),
        "counters": touch_ends(jax.random.randint(seeds[11], (POP,), 0, 1073741824), jax.random.fold_in(seeds[11], 1), 0, 1073741823).astype(jnp.int32),
        "fitness_rank": jax.random.permutation(seeds[12], POP).astype(jnp.int32),
    }


sigma_rate = 0.3
spread_rate = 0.4
single_rate = 0.1
collect_rate = 0.3
damping = 0.3
rope_base = 500000.0
epsilon = 1e-05
rotation_table = ((13, 15, 26, 6), (17, 29, 16, 24))

def rotate_left(word_value, distance):
    shifted = jnp.left_shift(word_value, jnp.int32(distance))
    wrapped = lax.shift_right_logical(word_value, jnp.full(word_value.shape, 32 - distance, jnp.int32))
    return jnp.bitwise_or(shifted, wrapped)

def threefry_words(key_word, block_word, pair_index):
    zero_word = jnp.zeros_like(key_word)
    third_key = jnp.bitwise_xor(key_word, jnp.int32(466688986))
    plan = (key_word, zero_word, third_key)
    leading = block_word + key_word
    trailing = pair_index + zero_word
    leading = leading + jnp.zeros_like(trailing)
    for group_round in range(5):
        for distance in rotation_table[group_round % 2]:
            leading = leading + trailing
            trailing = rotate_left(trailing, distance)
            trailing = jnp.bitwise_xor(trailing, leading)
        leading = leading + plan[(group_round + 1) % 3]
        trailing = trailing + plan[(group_round + 2) % 3] + jnp.int32(group_round + 1)
    return (leading, trailing)

def gaussian_pair(leading, trailing):
    unit_step = 2.0 ** (-23)
    shift_nine = jnp.full(leading.shape, 9, jnp.int32)
    uniform_part = (lax.shift_right_logical(leading, shift_nine) + 1).astype(jnp.float32) * unit_step
    angles = lax.shift_right_logical(trailing, shift_nine).astype(jnp.float32) * (2.0 * math.pi * unit_step)
    radius = jnp.sqrt(-2.0 * jnp.log(uniform_part))
    return (radius * jnp.cos(angles), radius * jnp.sin(angles))

def rank_weights(fitness_rank):
    amount = fitness_rank.shape[0]
    ceiling = math.log(2.0 * amount)
    levels = ceiling - jnp.log((lax.iota(jnp.int32, amount) + 1).astype(jnp.float32))
    weights = (ceiling - jnp.log((fitness_rank + 1).astype(jnp.float32))) / jnp.sum(levels)
    return (weights, 1.0 / jnp.sum(weights * weights))

def rotary(head_vectors, positions):
    half_width = head_vectors.shape[-1] // 2
    exponents = lax.iota(jnp.int32, half_width).astype(jnp.float32) * (-2.0 / head_vectors.shape[-1])
    frequency = jnp.power(jnp.float32(rope_base), exponents)
    phases = positions.astype(jnp.float32)[:, None] * frequency[None, :]
    cosine = jnp.cos(phases)[:, None, :]
    sine_part = jnp.sin(phases)[:, None, :]
    former = head_vectors[..., :half_width]
    latter = head_vectors[..., half_width:]
    return jnp.concatenate([former * cosine - latter * sine_part, latter * cosine + former * sine_part], axis=-1)

def attend(queries, keys, values, positions, sequences):
    row_count, state_heads, head_size = keys.shape
    grouped = queries.reshape(row_count, state_heads, -1, head_size).astype(jnp.float32)
    scores = jnp.einsum('tkgd,skd->kgts', grouped, keys.astype(jnp.float32), precision=lax.Precision.HIGHEST)
    scores = scores * head_size ** (-0.5)
    allowed = (sequences[:, None] == sequences[None, :]) & (positions[None, :] <= positions[:, None])
    scores = jnp.where(allowed, scores, jnp.float32(-1e+30))
    maximum = lax.optimization_barrier(jnp.max(scores, axis=-1, keepdims=True))
    lifted = jnp.exp(scores - maximum)
    attention = (lifted / lax.optimization_barrier(jnp.sum(lifted, axis=-1, keepdims=True))).astype(jnp.bfloat16)
    context = jnp.einsum('kgts,skd->tkgd', attention.astype(jnp.float32), values.astype(jnp.float32), precision=lax.Precision.HIGHEST)
    return context.astype(jnp.bfloat16).reshape(row_count, -1)

def reference(tokens, embedding, norm_gain, query_weight, out_weight, center, variance, step_path, spread_path, step_size, noise_seeds, counters, fitness_rank):
    token_ids = tokens.reshape(-1)
    row_count = token_ids.shape[0]
    hidden = jnp.take(embedding, token_ids, axis=0)
    hidden_wide = hidden.astype(jnp.float32)
    normed = (hidden_wide * lax.rsqrt(lax.optimization_barrier(jnp.mean(hidden_wide * hidden_wide, axis=1, keepdims=True)) + epsilon) * norm_gain).astype(jnp.bfloat16)
    positions = lax.iota(jnp.int32, row_count) % LEN
    sequences = lax.iota(jnp.int32, row_count) // LEN
    projected = jnp.dot(normed, query_weight, preferred_element_type=jnp.float32).reshape(row_count, HQ, HD)
    queries = rotary(projected, positions).astype(jnp.bfloat16)
    weights, effective = rank_weights(fitness_rank)
    spread_root = jnp.sqrt(variance)
    step_value = step_size[0]
    pair_index = lax.broadcasted_iota(jnp.int32, (D, KVW), 0) * KVW + lax.broadcasted_iota(jnp.int32, (D, KVW), 1)
    head_cols = QW // N_TP

    def evaluate(running, inputs):
        mean_noise, square_noise = running
        seed_word, counter_word, weight_value = inputs
        leading, trailing = threefry_words(seed_word, counter_word, pair_index)
        cosine_part, sine_part = gaussian_pair(leading, trailing)
        perturb = jnp.stack([cosine_part, sine_part])
        candidate = ((center + step_value * spread_root * perturb) * D ** (-0.5)).astype(jnp.bfloat16)
        keys = jnp.dot(normed, candidate[0], preferred_element_type=jnp.float32).reshape(row_count, KV, HD)
        keys = rotary(keys, positions).astype(jnp.bfloat16)
        values = jnp.dot(normed, candidate[1], preferred_element_type=jnp.float32).astype(jnp.bfloat16).reshape(row_count, KV, HD)
        context = attend(queries, keys, values, positions, sequences)
        partials = jnp.einsum('tgc,gcd->gtd', context.reshape(row_count, N_TP, head_cols).astype(jnp.float32), out_weight.reshape(N_TP, head_cols, D).astype(jnp.float32), precision=lax.Precision.HIGHEST)
        partials = lax.optimization_barrier(partials.astype(jnp.bfloat16)).astype(jnp.float32)
        output = (hidden_wide + lax.optimization_barrier(jnp.sum(partials, axis=0))).astype(jnp.bfloat16)
        return ((mean_noise + weight_value * perturb, square_noise + weight_value * perturb * perturb), output)
    initial = jnp.zeros((2, D, KVW), jnp.float32)
    (mean_noise, square_noise), candidate_out = lax.scan(evaluate, (initial, initial), (noise_seeds, counters, weights))
    center_next = center + step_value * spread_root * mean_noise
    step_path_next = (1.0 - sigma_rate) * step_path + jnp.sqrt(sigma_rate * (2.0 - sigma_rate) * effective) * mean_noise
    spread_path_next = (1.0 - spread_rate) * spread_path + jnp.sqrt(spread_rate * (2.0 - spread_rate) * effective) * spread_root * mean_noise
    variance_next = (1.0 - single_rate - collect_rate) * variance + single_rate * spread_path_next * spread_path_next + collect_rate * variance * square_noise
    squares = jnp.sum(step_path_next * step_path_next)
    step_next = step_size * jnp.exp(sigma_rate / (2.0 * damping) * (squares / (2.0 * D * KVW) - 1.0))
    return (candidate_out, center_next, variance_next, step_path_next, spread_path_next, step_next)
```

```python
import functools
import math

import jax
import jax.numpy as jnp
from jax import lax
from jax.experimental import pallas as pl
from jax.experimental.pallas import tpu as pltpu
from jax.sharding import PartitionSpec as P

HD = 128


sigma_rate = 0.3
spread_rate = 0.4
single_rate = 0.1
collect_rate = 0.3
damping = 0.3
rope_base = 500000.0
epsilon = 1e-05
rotation_table = ((13, 15, 26, 6), (17, 29, 16, 24))


def rotate_left(word_value, distance):
    shifted = jnp.left_shift(word_value, jnp.int32(distance))
    wrapped = lax.shift_right_logical(
        word_value, jnp.full(word_value.shape, 32 - distance, jnp.int32)
    )
    return jnp.bitwise_or(shifted, wrapped)


def threefry_words(key_word, block_word, pair_index):
    zero_word = jnp.zeros_like(key_word)
    third_key = jnp.bitwise_xor(key_word, jnp.int32(466688986))
    plan = (key_word, zero_word, third_key)
    leading = block_word + key_word
    trailing = pair_index + zero_word
    leading = leading + jnp.zeros_like(trailing)
    for group_round in range(5):
        for distance in rotation_table[group_round % 2]:
            leading = leading + trailing
            trailing = rotate_left(trailing, distance)
            trailing = jnp.bitwise_xor(trailing, leading)
        leading = leading + plan[(group_round + 1) % 3]
        trailing = trailing + plan[(group_round + 2) % 3] + jnp.int32(group_round + 1)
    return (leading, trailing)


def gaussian_pair(leading, trailing):
    unit_step = 2.0 ** (-23)
    shift_nine = jnp.full(leading.shape, 9, jnp.int32)
    uniform_part = (lax.shift_right_logical(leading, shift_nine) + 1).astype(
        jnp.float32
    ) * unit_step
    angles = lax.shift_right_logical(trailing, shift_nine).astype(jnp.float32) * (
        2.0 * math.pi * unit_step
    )
    radius = jnp.sqrt(-2.0 * jnp.log(uniform_part))
    return (radius * jnp.cos(angles), radius * jnp.sin(angles))


def rank_weights(fitness_rank):
    amount = fitness_rank.shape[0]
    ceiling = math.log(2.0 * amount)
    levels = ceiling - jnp.log((lax.iota(jnp.int32, amount) + 1).astype(jnp.float32))
    weights = (ceiling - jnp.log((fitness_rank + 1).astype(jnp.float32))) / jnp.sum(levels)
    return (weights, 1.0 / jnp.sum(weights * weights))


MESH = pl.DeviceIdType.MESH
VMEM_BYTES = 56 * 1024 * 1024


def rotary_tables(positions):
    half_width = HD // 2
    exponents = lax.iota(jnp.int32, half_width).astype(jnp.float32) * (-2.0 / HD)
    frequency = jnp.power(jnp.float32(rope_base), exponents)
    phases = positions.astype(jnp.float32)[:, None] * frequency[None, :]
    cosine = jnp.cos(phases)
    sine_part = jnp.sin(phases)
    return (
        jnp.concatenate([cosine, cosine], axis=1),
        jnp.concatenate([-sine_part, sine_part], axis=1),
    )


def sum_kernel(size, x_ref, out_ref, landed, reduced, send_a, recv_a, send_b, recv_b):
    me = lax.axis_index("pop")
    barrier = pltpu.get_barrier_semaphore()
    for j in range(1, size):
        pl.semaphore_signal(
            barrier, inc=1, device_id={"pop": lax.rem(me + j, size)}, device_id_type=MESH
        )
    pl.semaphore_wait(barrier, size - 1)
    copies = []
    for j in range(1, size):
        peer = lax.rem(me + j, size)
        copy = pltpu.make_async_remote_copy(
            src_ref=x_ref.at[peer],
            dst_ref=landed.at[j],
            send_sem=send_a.at[j],
            recv_sem=recv_a.at[j],
            device_id={"pop": peer},
            device_id_type=MESH,
        )
        copy.start()
        copies.append(copy)
    total = x_ref[me].astype(jnp.float32)
    for j in range(1, size):
        copies[j - 1].wait_recv()
        total = total + landed[j].astype(jnp.float32)
    reduced[...] = total.astype(jnp.bfloat16)
    later = []
    for j in range(1, size):
        peer = lax.rem(me + j, size)
        copy = pltpu.make_async_remote_copy(
            src_ref=reduced,
            dst_ref=out_ref.at[me],
            send_sem=send_b.at[j],
            recv_sem=recv_b.at[j],
            device_id={"pop": peer},
            device_id_type=MESH,
        )
        copy.start()
        later.append(copy)
    out_ref[me] = reduced[...]
    for copy in copies:
        copy.wait_send()
    for copy in later:
        copy.wait_recv()
    for copy in later:
        copy.wait_send()


def sum_over_pop(parts, size):
    _, rows, width = parts.shape
    return pl.pallas_call(
        functools.partial(sum_kernel, size),
        out_shape=jax.ShapeDtypeStruct(parts.shape, jnp.bfloat16),
        in_specs=[pl.BlockSpec(memory_space=pltpu.VMEM)],
        out_specs=pl.BlockSpec(memory_space=pltpu.VMEM),
        scratch_shapes=[
            pltpu.VMEM((size, rows, width), jnp.bfloat16),
            pltpu.VMEM((rows, width), jnp.bfloat16),
            pltpu.SemaphoreType.DMA((size,)),
            pltpu.SemaphoreType.DMA((size,)),
            pltpu.SemaphoreType.DMA((size,)),
            pltpu.SemaphoreType.DMA((size,)),
        ],
        compiler_params=pltpu.CompilerParams(
            collective_id=1, has_side_effects=True, vmem_limit_bytes=VMEM_BYTES
        ),
        name="sum_over_pop",
    )(parts)


def attend_kernel(length, q_ref, k_ref, v_ref, cos_ref, sin_ref, out_ref, turned):
    rows = q_ref.shape[0]
    heads = q_ref.shape[1] // HD
    states = k_ref.shape[2] // HD
    group = heads // states
    cosine = cos_ref[...]
    sine = sin_ref[...]

    def turn(x):
        return (x * cosine + pltpu.roll(x, HD // 2, 1) * sine).astype(jnp.bfloat16)

    @pl.when(pl.program_id(0) == 0)
    def _():
        for h in range(heads):
            turned[h] = turn(q_ref[:, h * HD : (h + 1) * HD].astype(jnp.float32))

    row = lax.broadcasted_iota(jnp.int32, (rows, rows), 0)
    col = lax.broadcasted_iota(jnp.int32, (rows, rows), 1)
    allowed = (row // length == col // length) & (col <= row)
    for g in range(states):
        keys = turn(k_ref[0, :, g * HD : (g + 1) * HD].astype(jnp.float32))
        values = v_ref[0, :, g * HD : (g + 1) * HD]
        queries = turned[g * group : (g + 1) * group].reshape(group * rows, HD)
        scores = lax.dot_general(
            queries, keys, (((1,), (1,)), ((), ())), preferred_element_type=jnp.float32
        ).reshape(group, rows, rows)
        scores = jnp.where(allowed[None], scores * HD ** (-0.5), jnp.float32(-1e30))
        lifted = jnp.exp(scores - jnp.max(scores, axis=-1, keepdims=True))
        attention = (lifted / jnp.sum(lifted, axis=-1, keepdims=True)).astype(jnp.bfloat16)
        context = jnp.dot(
            attention.reshape(group * rows, rows), values, preferred_element_type=jnp.float32
        ).astype(jnp.bfloat16)
        for i in range(group):
            h = g * group + i
            out_ref[0, :, h * HD : (h + 1) * HD] = context[i * rows : (i + 1) * rows]


def attend_all(queries, keys, values, cosine, sine, length):
    size, rows, width = keys.shape
    q_cols = queries.shape[1]

    def whole(shape):
        return pl.BlockSpec(shape, lambda k: (0,) * len(shape))

    return pl.pallas_call(
        functools.partial(attend_kernel, length),
        grid=(size,),
        out_shape=jax.ShapeDtypeStruct((size, rows, q_cols), jnp.bfloat16),
        in_specs=[
            whole((rows, q_cols)),
            pl.BlockSpec((1, rows, width), lambda k: (k, 0, 0)),
            pl.BlockSpec((1, rows, width), lambda k: (k, 0, 0)),
            whole((rows, HD)),
            whole((rows, HD)),
        ],
        out_specs=pl.BlockSpec((1, rows, q_cols), lambda k: (k, 0, 0)),
        scratch_shapes=[pltpu.VMEM((q_cols // HD, rows, HD), jnp.bfloat16)],
        compiler_params=pltpu.CompilerParams(vmem_limit_bytes=VMEM_BYTES),
        name="attend_all",
    )(queries, keys, values, cosine, sine)


def output_kernel(
    size, heads, c_ref, w_ref, r_ref, o_ref, part, landed, final, arrived, sa, ra, sb, rb
):
    me = lax.axis_index("pop")
    head = lax.axis_index("tp")
    each = size // heads
    rows, width = r_ref.shape
    home = me // each
    barrier = pltpu.get_barrier_semaphore()
    for j in range(1, heads):
        pl.semaphore_signal(
            barrier,
            inc=1,
            device_id=(me, lax.rem(head + j, heads)),
            device_id_type=MESH,
        )
    for s in range(1, each):
        pl.semaphore_signal(
            barrier,
            inc=1,
            device_id=(each * head + lax.rem(me + s, each), home),
            device_id_type=MESH,
        )

    @pl.when(home != head)
    def _():
        pl.semaphore_signal(
            barrier,
            inc=1,
            device_id=(each * head + lax.rem(me, each), home),
            device_id_type=MESH,
        )
        pl.semaphore_wait(barrier, heads - 1 + each)

    @pl.when(home == head)
    def _():
        pl.semaphore_wait(barrier, heads - 1 + each - 1)

    def product(h):
        block = c_ref[pl.ds(h * each, each)].reshape(each * rows, c_ref.shape[2])
        return jnp.dot(block, w_ref[...], preferred_element_type=jnp.float32).astype(
            jnp.bfloat16
        )

    order = sorted(range(1, heads), key=lambda j: abs(j - heads // 2))
    copies = {}
    for j in order:
        peer = lax.rem(head + j, heads)
        part[j] = product(peer).reshape(each, rows, width)
        copies[j] = pltpu.make_async_remote_copy(
            src_ref=part.at[j],
            dst_ref=landed.at[j],
            send_sem=sa.at[j],
            recv_sem=ra.at[j],
            device_id=(me, peer),
            device_id_type=MESH,
        )
        copies[j].start()
    part[0] = product(head).reshape(each, rows, width)
    for j in order:
        copies[j].wait_recv()
    residual = r_ref[...].astype(jnp.float32)
    finals = []
    for s in range(each):
        i = lax.rem(me + s, each)
        total = part[0, i].astype(jnp.float32)
        for j in range(1, heads):
            total = total + landed[j, i].astype(jnp.float32)
        final[s] = (total + residual).astype(jnp.bfloat16)
        copy = pltpu.make_async_remote_copy(
            src_ref=final.at[s],
            dst_ref=arrived.at[s],
            send_sem=sb.at[s],
            recv_sem=rb.at[s],
            device_id=(each * head + i, home),
            device_id_type=MESH,
        )
        finals.append(copy)
        if s == 0:

            @pl.when(home != head)
            def _():
                finals[0].start()

        else:
            copy.start()
    for j in order:
        copies[j].wait_send()
    for s in range(1, each):
        finals[s].wait()

    @pl.when(home != head)
    def _():
        finals[0].wait()

    @pl.when(home == head)
    def _():
        arrived[0] = final[0]

    for c in range(each):
        s = lax.rem(me - c + each * size, each)
        o_ref[:, c * width : (c + 1) * width] = arrived[s]


def output_sum(context, out_weight, residual, size, heads):
    each = size // heads
    rows, width = residual.shape
    return pl.pallas_call(
        functools.partial(output_kernel, size, heads),
        out_shape=jax.ShapeDtypeStruct((rows, each * width), jnp.bfloat16),
        in_specs=[pl.BlockSpec(memory_space=pltpu.VMEM)] * 3,
        out_specs=pl.BlockSpec(memory_space=pltpu.VMEM),
        scratch_shapes=[
            pltpu.VMEM((heads, each, rows, width), jnp.bfloat16),
            pltpu.VMEM((heads, each, rows, width), jnp.bfloat16),
            pltpu.VMEM((each, rows, width), jnp.bfloat16),
            pltpu.VMEM((each, rows, width), jnp.bfloat16),
            pltpu.SemaphoreType.DMA((heads,)),
            pltpu.SemaphoreType.DMA((heads,)),
            pltpu.SemaphoreType.DMA((each,)),
            pltpu.SemaphoreType.DMA((each,)),
        ],
        compiler_params=pltpu.CompilerParams(
            collective_id=2, has_side_effects=True, vmem_limit_bytes=VMEM_BYTES
        ),
        name="output_sum",
    )(context, out_weight, residual)


def on_device(
    tokens,
    embedding,
    norm_gain,
    query_weight,
    out_weight,
    center,
    variance,
    step_path,
    spread_path,
    step_size,
    noise_seeds,
    counters,
    fitness_rank,
):
    group_index = lax.axis_index("pop")
    head_index = lax.axis_index("tp")
    head_count = lax.axis_size("tp")
    seq_count, seq_length = tokens.shape
    row_count = seq_count * seq_length
    token_ids = tokens.reshape(row_count)
    positions = lax.iota(jnp.int32, row_count) % seq_length
    model_width = embedding.shape[1]
    shard_rows = center.shape[1]
    shard_cols = center.shape[2]
    state_width = shard_cols * head_count
    row_ids = group_index * shard_rows + lax.iota(jnp.int32, shard_rows)
    col_ids = head_index * shard_cols + lax.iota(jnp.int32, shard_cols)
    pair_index = row_ids[:, None] * state_width + col_ids[None, :]
    leading, trailing = threefry_words(
        noise_seeds[:, None, None], counters[:, None, None], pair_index[None]
    )
    cosine_part, sine_part = gaussian_pair(leading, trailing)
    perturb = jnp.stack([cosine_part, sine_part], axis=1)
    weights, effective = rank_weights(fitness_rank)
    spread_root = jnp.sqrt(variance)
    step_value = step_size[0]
    candidates = (
        (center[None] + step_value * spread_root[None] * perturb) * model_width ** (-0.5)
    ).astype(jnp.bfloat16)
    weighted = weights[:, None, None, None]
    mean_noise = jnp.sum(weighted * perturb, axis=0)
    square_noise = jnp.sum(weighted * perturb * perturb, axis=0)
    center_next = center + step_value * spread_root * mean_noise
    step_path_next = (1.0 - sigma_rate) * step_path + jnp.sqrt(
        sigma_rate * (2.0 - sigma_rate) * effective
    ) * mean_noise
    spread_path_next = (1.0 - spread_rate) * spread_path + jnp.sqrt(
        spread_rate * (2.0 - spread_rate) * effective
    ) * spread_root * mean_noise
    variance_next = (
        (1.0 - single_rate - collect_rate) * variance
        + single_rate * spread_path_next * spread_path_next
        + collect_rate * variance * square_noise
    )
    norm_local = jnp.sum(step_path_next * step_path_next)
    vocab_rows = embedding.shape[0]
    local_ids = token_ids - (group_index * head_count + head_index) * vocab_rows
    inside = (local_ids >= 0) & (local_ids < vocab_rows)
    picked = jnp.take(embedding, jnp.clip(local_ids, 0, vocab_rows - 1), axis=0)
    picked = jnp.where(inside[:, None], picked, jnp.zeros_like(picked))
    picked_wide = picked.astype(jnp.float32)
    squares = jnp.sum(picked_wide * picked_wide, axis=1)
    pop_size = lax.axis_size("pop")
    cut = picked.reshape(row_count, pop_size, head_count, -1).transpose(2, 1, 0, 3)
    cut = lax.psum_scatter(cut, "tp", scatter_dimension=0, tiled=False)
    cut = lax.psum_scatter(cut, "pop", scatter_dimension=0, tiled=False)
    hidden = lax.all_gather(cut, "tp", axis=0).transpose(1, 0, 2).reshape(row_count, shard_rows)
    squares = lax.psum(squares, ("pop", "tp"))
    norm_local, squares = lax.optimization_barrier((norm_local, squares))
    norm_total = lax.psum(norm_local, ("pop", "tp"))
    own_gain = lax.dynamic_slice_in_dim(norm_gain, group_index * shard_rows, shard_rows, 0)
    own_rows = (
        hidden.astype(jnp.float32)
        * lax.rsqrt(squares / model_width + epsilon)[:, None]
        * own_gain
    ).astype(jnp.bfloat16)
    query_cols = query_weight.shape[1]
    query_cut = query_cols // pop_size
    query_part = jnp.dot(own_rows, query_weight, preferred_element_type=jnp.float32)
    query_part = query_part.astype(jnp.bfloat16).reshape(row_count, pop_size, query_cut)
    state_part = jnp.einsum(
        "td,kmdc->kmtc", own_rows, candidates, preferred_element_type=jnp.float32
    ).astype(jnp.bfloat16)
    summed = sum_over_pop(
        jnp.concatenate(
            [state_part[:, 0], state_part[:, 1], query_part.transpose(1, 0, 2)], axis=2
        ),
        pop_size,
    )
    queries = summed[:, :, 2 * shard_cols :].transpose(1, 0, 2).reshape(row_count, query_cols)
    cosine_table, sine_table = rotary_tables(positions)
    context = attend_all(
        queries,
        summed[:, :, :shard_cols],
        summed[:, :, shard_cols : 2 * shard_cols],
        cosine_table,
        sine_table,
        seq_length,
    )
    candidate_out = output_sum(context, out_weight, hidden, pop_size, head_count)[None]
    total_params = 2.0 * model_width * state_width
    step_next = step_size * jnp.exp(
        sigma_rate / (2.0 * damping) * (norm_total / total_params - 1.0)
    )
    return (candidate_out, center_next, variance_next, step_path_next, spread_path_next, step_next)


def solution(mesh):
    placed = (
        P(),
        P(("pop", "tp"), None),
        P(),
        P("pop", "tp"),
        P("tp", "pop"),
        P(None, "pop", "tp"),
        P(None, "pop", "tp"),
        P(None, "pop", "tp"),
        P(None, "pop", "tp"),
        P(),
        P(),
        P(),
        P(),
    )
    return jax.shard_map(
        on_device,
        mesh=mesh,
        in_specs=placed,
        out_specs=(
            P("pop", None, "tp"),
            P(None, "pop", "tp"),
            P(None, "pop", "tp"),
            P(None, "pop", "tp"),
            P(None, "pop", "tp"),
            P(),
        ),
        check_vma=False,
    )
```

```python
import functools
import math

import jax
import jax.numpy as jnp
from jax import lax
from jax.experimental import pallas as pl
from jax.experimental.pallas import tpu as pltpu
from jax.sharding import PartitionSpec as P

HD = 128


sigma_rate = 0.3
spread_rate = 0.4
single_rate = 0.1
collect_rate = 0.3
damping = 0.3
rope_base = 500000.0
epsilon = 1e-05
rotation_table = ((13, 15, 26, 6), (17, 29, 16, 24))


def rotate_left(word_value, distance):
    shifted = jnp.left_shift(word_value, jnp.int32(distance))
    wrapped = lax.shift_right_logical(
        word_value, jnp.full(word_value.shape, 32 - distance, jnp.int32)
    )
    return jnp.bitwise_or(shifted, wrapped)


def threefry_words(key_word, block_word, pair_index):
    zero_word = jnp.zeros_like(key_word)
    third_key = jnp.bitwise_xor(key_word, jnp.int32(466688986))
    plan = (key_word, zero_word, third_key)
    leading = block_word + key_word
    trailing = pair_index + zero_word
    leading = leading + jnp.zeros_like(trailing)
    for group_round in range(5):
        for distance in rotation_table[group_round % 2]:
            leading = leading + trailing
            trailing = rotate_left(trailing, distance)
            trailing = jnp.bitwise_xor(trailing, leading)
        leading = leading + plan[(group_round + 1) % 3]
        trailing = trailing + plan[(group_round + 2) % 3] + jnp.int32(group_round + 1)
    return (leading, trailing)


def gaussian_pair(leading, trailing):
    unit_step = 2.0 ** (-23)
    shift_nine = jnp.full(leading.shape, 9, jnp.int32)
    uniform_part = (lax.shift_right_logical(leading, shift_nine) + 1).astype(
        jnp.float32
    ) * unit_step
    angles = lax.shift_right_logical(trailing, shift_nine).astype(jnp.float32) * (
        2.0 * math.pi * unit_step
    )
    radius = jnp.sqrt(-2.0 * jnp.log(uniform_part))
    return (radius * jnp.cos(angles), radius * jnp.sin(angles))


def rank_weights(fitness_rank):
    amount = fitness_rank.shape[0]
    ceiling = math.log(2.0 * amount)
    levels = ceiling - jnp.log((lax.iota(jnp.int32, amount) + 1).astype(jnp.float32))
    weights = (ceiling - jnp.log((fitness_rank + 1).astype(jnp.float32))) / jnp.sum(levels)
    return (weights, 1.0 / jnp.sum(weights * weights))


MESH = pl.DeviceIdType.MESH
VMEM_BYTES = 56 * 1024 * 1024


def rotary_tables(positions):
    half_width = HD // 2
    exponents = lax.iota(jnp.int32, half_width).astype(jnp.float32) * (-2.0 / HD)
    frequency = jnp.power(jnp.float32(rope_base), exponents)
    phases = positions.astype(jnp.float32)[:, None] * frequency[None, :]
    cosine = jnp.cos(phases)
    sine_part = jnp.sin(phases)
    return (
        jnp.concatenate([cosine, cosine], axis=1),
        jnp.concatenate([-sine_part, sine_part], axis=1),
    )


def sum_kernel(size, x_ref, out_ref, landed, reduced, send_a, recv_a, send_b, recv_b):
    me = lax.axis_index("pop")
    barrier = pltpu.get_barrier_semaphore()
    for j in range(1, size):
        pl.semaphore_signal(
            barrier, inc=1, device_id={"pop": lax.rem(me + j, size)}, device_id_type=MESH
        )
    pl.semaphore_wait(barrier, size - 1)
    copies = []
    for j in range(1, size):
        peer = lax.rem(me + j, size)
        copy = pltpu.make_async_remote_copy(
            src_ref=x_ref.at[peer],
            dst_ref=landed.at[j],
            send_sem=send_a.at[j],
            recv_sem=recv_a.at[j],
            device_id={"pop": peer},
            device_id_type=MESH,
        )
        copy.start()
        copies.append(copy)
    total = x_ref[me].astype(jnp.float32)
    for j in range(1, size):
        copies[j - 1].wait_recv()
        total = total + landed[j].astype(jnp.float32)
    reduced[...] = total.astype(jnp.bfloat16)
    later = []
    for j in range(1, size):
        peer = lax.rem(me + j, size)
        copy = pltpu.make_async_remote_copy(
            src_ref=reduced,
            dst_ref=out_ref.at[me],
            send_sem=send_b.at[j],
            recv_sem=recv_b.at[j],
            device_id={"pop": peer},
            device_id_type=MESH,
        )
        copy.start()
        later.append(copy)
    out_ref[me] = reduced[...]
    for copy in copies:
        copy.wait_send()
    for copy in later:
        copy.wait_recv()
    for copy in later:
        copy.wait_send()


def sum_over_pop(parts, size):
    _, rows, width = parts.shape
    return pl.pallas_call(
        functools.partial(sum_kernel, size),
        out_shape=jax.ShapeDtypeStruct(parts.shape, jnp.bfloat16),
        in_specs=[pl.BlockSpec(memory_space=pltpu.VMEM)],
        out_specs=pl.BlockSpec(memory_space=pltpu.VMEM),
        scratch_shapes=[
            pltpu.VMEM((size, rows, width), jnp.bfloat16),
            pltpu.VMEM((rows, width), jnp.bfloat16),
            pltpu.SemaphoreType.DMA((size,)),
            pltpu.SemaphoreType.DMA((size,)),
            pltpu.SemaphoreType.DMA((size,)),
            pltpu.SemaphoreType.DMA((size,)),
        ],
        compiler_params=pltpu.CompilerParams(
            collective_id=1, has_side_effects=True, vmem_limit_bytes=VMEM_BYTES
        ),
        name="sum_over_pop",
    )(parts)


def attend_kernel(length, q_ref, k_ref, v_ref, cos_ref, sin_ref, out_ref, turned):
    rows = q_ref.shape[0]
    heads = q_ref.shape[1] // HD
    states = k_ref.shape[2] // HD
    group = heads // states
    cosine = cos_ref[...]
    sine = sin_ref[...]

    def turn(x):
        return (x * cosine + pltpu.roll(x, HD // 2, 1) * sine).astype(jnp.bfloat16)

    @pl.when(pl.program_id(0) == 0)
    def _():
        for h in range(heads):
            turned[h] = turn(q_ref[:, h * HD : (h + 1) * HD].astype(jnp.float32))

    row = lax.broadcasted_iota(jnp.int32, (rows, rows), 0)
    col = lax.broadcasted_iota(jnp.int32, (rows, rows), 1)
    allowed = (row // length == col // length) & (col <= row)
    for g in range(states):
        keys = turn(k_ref[0, :, g * HD : (g + 1) * HD].astype(jnp.float32))
        values = v_ref[0, :, g * HD : (g + 1) * HD]
        queries = turned[g * group : (g + 1) * group].reshape(group * rows, HD)
        scores = lax.dot_general(
            queries, keys, (((1,), (1,)), ((), ())), preferred_element_type=jnp.float32
        ).reshape(group, rows, rows)
        scores = jnp.where(allowed[None], scores * HD ** (-0.5), jnp.float32(-1e30))
        lifted = jnp.exp(scores - jnp.max(scores, axis=-1, keepdims=True))
        attention = (lifted / jnp.sum(lifted, axis=-1, keepdims=True)).astype(jnp.bfloat16)
        context = jnp.dot(
            attention.reshape(group * rows, rows), values, preferred_element_type=jnp.float32
        ).astype(jnp.bfloat16)
        for i in range(group):
            h = g * group + i
            out_ref[0, :, h * HD : (h + 1) * HD] = context[i * rows : (i + 1) * rows]


def attend_all(queries, keys, values, cosine, sine, length):
    size, rows, width = keys.shape
    q_cols = queries.shape[1]

    def whole(shape):
        return pl.BlockSpec(shape, lambda k: (0,) * len(shape))

    return pl.pallas_call(
        functools.partial(attend_kernel, length),
        grid=(size,),
        out_shape=jax.ShapeDtypeStruct((size, rows, q_cols), jnp.bfloat16),
        in_specs=[
            whole((rows, q_cols)),
            pl.BlockSpec((1, rows, width), lambda k: (k, 0, 0)),
            pl.BlockSpec((1, rows, width), lambda k: (k, 0, 0)),
            whole((rows, HD)),
            whole((rows, HD)),
        ],
        out_specs=pl.BlockSpec((1, rows, q_cols), lambda k: (k, 0, 0)),
        scratch_shapes=[pltpu.VMEM((q_cols // HD, rows, HD), jnp.bfloat16)],
        compiler_params=pltpu.CompilerParams(vmem_limit_bytes=VMEM_BYTES),
        name="attend_all",
    )(queries, keys, values, cosine, sine)


def output_kernel(
    size, heads, c_ref, w_ref, r_ref, o_ref, part, landed, final, arrived, sa, ra, sb, rb
):
    me = lax.axis_index("pop")
    head = lax.axis_index("tp")
    each = size // heads
    rows, width = r_ref.shape
    home = me // each
    barrier = pltpu.get_barrier_semaphore()
    for j in range(1, heads):
        pl.semaphore_signal(
            barrier,
            inc=1,
            device_id=(me, lax.rem(head + j, heads)),
            device_id_type=MESH,
        )
    for s in range(1, each):
        pl.semaphore_signal(
            barrier,
            inc=1,
            device_id=(each * head + lax.rem(me + s, each), home),
            device_id_type=MESH,
        )

    @pl.when(home != head)
    def _():
        pl.semaphore_signal(
            barrier,
            inc=1,
            device_id=(each * head + lax.rem(me, each), home),
            device_id_type=MESH,
        )
        pl.semaphore_wait(barrier, heads - 1 + each)

    @pl.when(home == head)
    def _():
        pl.semaphore_wait(barrier, heads - 1 + each - 1)

    def product(h):
        block = c_ref[pl.ds(h * each, each)].reshape(each * rows, c_ref.shape[2])
        return jnp.dot(block, w_ref[...], preferred_element_type=jnp.float32).astype(
            jnp.bfloat16
        )

    order = sorted(range(1, heads), key=lambda j: abs(j - heads // 2))
    copies = {}
    for j in order:
        peer = lax.rem(head + j, heads)
        part[j] = product(peer).reshape(each, rows, width)
        copies[j] = pltpu.make_async_remote_copy(
            src_ref=part.at[j],
            dst_ref=landed.at[j],
            send_sem=sa.at[j],
            recv_sem=ra.at[j],
            device_id=(me, peer),
            device_id_type=MESH,
        )
        copies[j].start()
    part[0] = product(head).reshape(each, rows, width)
    for j in order:
        copies[j].wait_recv()
    residual = r_ref[...].astype(jnp.float32)
    finals = []
    for s in range(each):
        i = lax.rem(me + s, each)
        total = part[0, i].astype(jnp.float32)
        for j in range(1, heads):
            total = total + landed[j, i].astype(jnp.float32)
        final[s] = (total + residual).astype(jnp.bfloat16)
        copy = pltpu.make_async_remote_copy(
            src_ref=final.at[s],
            dst_ref=arrived.at[s],
            send_sem=sb.at[s],
            recv_sem=rb.at[s],
            device_id=(each * head + i, home),
            device_id_type=MESH,
        )
        finals.append(copy)
        if s == 0:

            @pl.when(home != head)
            def _():
                finals[0].start()

        else:
            copy.start()
    for j in order:
        copies[j].wait_send()
    for s in range(1, each):
        finals[s].wait()

    @pl.when(home != head)
    def _():
        finals[0].wait()

    @pl.when(home == head)
    def _():
        arrived[0] = final[0]

    for c in range(each):
        s = lax.rem(me - c + each * size, each)
        o_ref[:, c * width : (c + 1) * width] = arrived[s]


def output_sum(context, out_weight, residual, size, heads):
    each = size // heads
    rows, width = residual.shape
    return pl.pallas_call(
        functools.partial(output_kernel, size, heads),
        out_shape=jax.ShapeDtypeStruct((rows, each * width), jnp.bfloat16),
        in_specs=[pl.BlockSpec(memory_space=pltpu.VMEM)] * 3,
        out_specs=pl.BlockSpec(memory_space=pltpu.VMEM),
        scratch_shapes=[
            pltpu.VMEM((heads, each, rows, width), jnp.bfloat16),
            pltpu.VMEM((heads, each, rows, width), jnp.bfloat16),
            pltpu.VMEM((each, rows, width), jnp.bfloat16),
            pltpu.VMEM((each, rows, width), jnp.bfloat16),
            pltpu.SemaphoreType.DMA((heads,)),
            pltpu.SemaphoreType.DMA((heads,)),
            pltpu.SemaphoreType.DMA((each,)),
            pltpu.SemaphoreType.DMA((each,)),
        ],
        compiler_params=pltpu.CompilerParams(
            collective_id=2, has_side_effects=True, vmem_limit_bytes=VMEM_BYTES
        ),
        name="output_sum",
    )(context, out_weight, residual)


def on_device(
    tokens,
    embedding,
    norm_gain,
    query_weight,
    out_weight,
    center,
    variance,
    step_path,
    spread_path,
    step_size,
    noise_seeds,
    counters,
    fitness_rank,
):
    group_index = lax.axis_index("pop")
    head_index = lax.axis_index("tp")
    head_count = lax.axis_size("tp")
    seq_count, seq_length = tokens.shape
    row_count = seq_count * seq_length
    token_ids = tokens.reshape(row_count)
    positions = lax.iota(jnp.int32, row_count) % seq_length
    model_width = embedding.shape[1]
    shard_rows = center.shape[1]
    shard_cols = center.shape[2]
    state_width = shard_cols * head_count
    row_ids = group_index * shard_rows + lax.iota(jnp.int32, shard_rows)
    col_ids = head_index * shard_cols + lax.iota(jnp.int32, shard_cols)
    pair_index = row_ids[:, None] * state_width + col_ids[None, :]
    leading, trailing = threefry_words(
        noise_seeds[:, None, None], counters[:, None, None], pair_index[None]
    )
    cosine_part, sine_part = gaussian_pair(leading, trailing)
    perturb = jnp.stack([cosine_part, sine_part], axis=1)
    weights, effective = rank_weights(fitness_rank)
    spread_root = jnp.sqrt(variance)
    step_value = step_size[0]
    candidates = (
        (center[None] + step_value * spread_root[None] * perturb) * model_width ** (-0.5)
    ).astype(jnp.bfloat16)
    weighted = weights[:, None, None, None]
    mean_noise = jnp.sum(weighted * perturb, axis=0)
    square_noise = jnp.sum(weighted * perturb * perturb, axis=0)
    center_next = center + step_value * spread_root * mean_noise
    step_path_next = (1.0 - sigma_rate) * step_path + jnp.sqrt(
        sigma_rate * (2.0 - sigma_rate) * effective
    ) * mean_noise
    spread_path_next = (1.0 - spread_rate) * spread_path + jnp.sqrt(
        spread_rate * (2.0 - spread_rate) * effective
    ) * spread_root * mean_noise
    variance_next = (
        (1.0 - single_rate - collect_rate) * variance
        + single_rate * spread_path_next * spread_path_next
        + collect_rate * variance * square_noise
    )
    norm_local = jnp.sum(step_path_next * step_path_next)
    vocab_rows = embedding.shape[0]
    local_ids = token_ids - (group_index * head_count + head_index) * vocab_rows
    inside = (local_ids >= 0) & (local_ids < vocab_rows)
    picked = jnp.take(embedding, jnp.clip(local_ids, 0, vocab_rows - 1), axis=0)
    picked = jnp.where(inside[:, None], picked, jnp.zeros_like(picked))
    picked_wide = picked.astype(jnp.float32)
    squares = jnp.sum(picked_wide * picked_wide, axis=1)
    pop_size = lax.axis_size("pop")
    cut = picked.reshape(row_count, pop_size, head_count, -1).transpose(2, 1, 0, 3)
    cut = lax.psum_scatter(cut, "tp", scatter_dimension=0, tiled=False)
    cut = lax.psum_scatter(cut, "pop", scatter_dimension=0, tiled=False)
    hidden = lax.all_gather(cut, "tp", axis=0).transpose(1, 0, 2).reshape(row_count, shard_rows)
    scalars = jnp.concatenate([squares, norm_local[None]])
    scalars = jnp.sum(lax.all_gather(scalars, ("pop", "tp"), axis=0), axis=0)
    squares, norm_total = scalars[:row_count], scalars[row_count]
    own_gain = lax.dynamic_slice_in_dim(norm_gain, group_index * shard_rows, shard_rows, 0)
    own_rows = (
        hidden.astype(jnp.float32)
        * lax.rsqrt(squares / model_width + epsilon)[:, None]
        * own_gain
    ).astype(jnp.bfloat16)
    query_cols = query_weight.shape[1]
    query_cut = query_cols // pop_size
    query_part = jnp.dot(own_rows, query_weight, preferred_element_type=jnp.float32)
    query_part = query_part.astype(jnp.bfloat16).reshape(row_count, pop_size, query_cut)
    state_part = jnp.einsum(
        "td,kmdc->kmtc", own_rows, candidates, preferred_element_type=jnp.float32
    ).astype(jnp.bfloat16)
    summed = sum_over_pop(
        jnp.concatenate(
            [state_part[:, 0], state_part[:, 1], query_part.transpose(1, 0, 2)], axis=2
        ),
        pop_size,
    )
    queries = summed[:, :, 2 * shard_cols :].transpose(1, 0, 2).reshape(row_count, query_cols)
    cosine_table, sine_table = rotary_tables(positions)
    context = attend_all(
        queries,
        summed[:, :, :shard_cols],
        summed[:, :, shard_cols : 2 * shard_cols],
        cosine_table,
        sine_table,
        seq_length,
    )
    candidate_out = output_sum(context, out_weight, hidden, pop_size, head_count)[None]
    total_params = 2.0 * model_width * state_width
    step_next = step_size * jnp.exp(
        sigma_rate / (2.0 * damping) * (norm_total / total_params - 1.0)
    )
    return (candidate_out, center_next, variance_next, step_path_next, spread_path_next, step_next)


def solution(mesh):
    placed = (
        P(),
        P(("pop", "tp"), None),
        P(),
        P("pop", "tp"),
        P("tp", "pop"),
        P(None, "pop", "tp"),
        P(None, "pop", "tp"),
        P(None, "pop", "tp"),
        P(None, "pop", "tp"),
        P(),
        P(),
        P(),
        P(),
    )
    return jax.shard_map(
        on_device,
        mesh=mesh,
        in_specs=placed,
        out_specs=(
            P("pop", None, "tp"),
            P(None, "pop", "tp"),
            P(None, "pop", "tp"),
            P(None, "pop", "tp"),
            P(None, "pop", "tp"),
            P(),
        ),
        check_vma=False,
    )
```
